128 devices in a mesh: row: 4 (over z), col: 8 (over y, core), cuts: 4 (over x).
Axes of the slice: x: 4, y: 4, z: 4, core: 2. Of those that a mesh axis runs over, the one named last changes fastest.
Arguments:
- t_amp: bfloat16 [3072, 32768], P('row', ('col', 'cuts')), may hold values from -1 to 1
- v_int: bfloat16 [3072, 32768], P('row', ('col', 'cuts')), may hold values from -0.03125 to 0.03125
- block_map: int32 [48, 512], P('row', ('col', 'cuts')), may hold values 0 or 1
Outputs:
- residual: float32 [3072, 32768], P('row', ('col', 'cuts'))
The draws below stay inside these ranges and needn't reach their ends.
Inputs may be any that keep to these rules, and one draw needn't show every extreme that they name: `block_map`: 0 or 1 for each pair of symmetry blocks.
All inputs are finite; a program needn't handle non-finite values.
Results may differ from the reference program's by a relative error of at most 0.0029.
Values may be sent and summed in bfloat16 or wider, within the bound.
A program may use at most 128 MiB of HBM per device.

```python
import jax
import jax.numpy as jnp

BLK = 64
ROWS = 3072
COLS = 32768


def plant(values, stream_key, least, largest):
    shape = values.shape
    index_at = [jax.random.randint(jax.random.fold_in(stream_key, axis), (), 0, shape[axis]) for axis in range(len(shape))]
    values = values.at[tuple(index_at)].set(least)
    longest = shape.index(max(shape))
    index_at[longest] = (index_at[longest] + 1) % shape[longest]
    return values.at[tuple(index_at)].set(largest)


def shard_levels(key, shape, pieces, smallest, high):
    loudness, own = 1.0, jax.random.fold_in(key, 6)
    for axis_at, shards_of in pieces:
        draws = jnp.exp(jax.random.uniform(jax.random.fold_in(own, axis_at), (shards_of,), jnp.float32, smallest / len(pieces), high / len(pieces)))
        loudness = loudness * jnp.repeat(draws, shape[axis_at] // shards_of).reshape([-1 if axis == axis_at else 1 for axis in range(len(shape))])
    return loudness


def centred(own_key, shape, scale, most, pieces=(), held_as=jnp.bfloat16):
    values = jax.random.normal(own_key, shape, jnp.float32) * scale
    if len(pieces) > 0:
        values = shard_levels(own_key, shape, pieces, -0.22, 0.18) * values
    return jnp.clip(values, min=-most, max=most).astype(held_as)


def setup_inputs(seed: int = 0) -> dict:
    arg_keys = jax.random.split(jax.random.key(seed), 4)
    t_amp = centred(arg_keys[0], (ROWS, COLS), 0.15, 1.0, ((0, 4), (1, 32)))
    v_int = centred(arg_keys[1], (ROWS, COLS), COLS ** -0.5, 0.03125, ((0, 4), (1, 32)))
    block_map = plant((jax.random.randint(arg_keys[2], (ROWS // BLK, COLS // BLK), 0, 2) < 1).astype(jnp.int32), jax.random.fold_in(arg_keys[2], 1), 0, 1)
    return {"t_amp": t_amp, "v_int": v_int, "block_map": block_map}


def apply_map(values, block_map):
    row_blocks, col_blocks = block_map.shape
    shaped = values.reshape(row_blocks, values.shape[0] // row_blocks, col_blocks, values.shape[1] // col_blocks)
    weights = block_map.astype(values.dtype)[:, None, :, None]
    return (shaped * weights).reshape(values.shape)


def reference(t_amp, v_int, block_map):
    masked_t = apply_map(t_amp, block_map)
    masked_v = apply_map(v_int, block_map)
    w_pair = jnp.dot(masked_t.astype(jnp.float32), masked_v.astype(jnp.float32).T).astype(jnp.bfloat16)
    result = jnp.dot(w_pair.astype(jnp.float32), masked_t.astype(jnp.float32))
    return apply_map(result, block_map)
```

```python
import functools

import jax
import jax.numpy as jnp
from jax import lax
from jax.experimental import pallas as pl
from jax.experimental.pallas import tpu as pltpu
from jax.sharding import PartitionSpec as P

MESH = pl.DeviceIdType.MESH
CH = 256
UN = 128
NT = (((1,), (1,)), ((), ()))


def kernel(ny, nx, t_ref, v_ref, m_ref, out_ref, tall, mv, mask, part, crecv, s1, r1, s2, r2, wp, wg, acc,
           ts, tr, cs, cr, as_, ar, bs, br, zs, zr, g1s, g1r, g2s, g2r, g3s, g3r):
    rows, cols = t_ref.shape
    half = cols // 2
    nj = rows // CH
    nu = rows // UN
    vh = rows // 2
    z = lax.axis_index("row")
    col = lax.axis_index("col")
    x = lax.axis_index("cuts")
    y = lax.div(col, 2)
    h = lax.rem(col, 2)

    def dev(dz=0, dy=0, dx=0, flip=False):
        hh = 1 - h if flip else h
        return (lax.rem(z + dz, 4), 2 * lax.rem(y + dy, ny) + hh, lax.rem(x + dx, nx))

    partners = [dev(dz=d) for d in (1, 2, 3)] + [dev(flip=True)]
    partners += [dev(dy=d) for d in range(1, ny)] + [dev(dx=d) for d in range(1, nx)]
    barrier = pltpu.get_barrier_semaphore()
    for p in partners:
        pl.semaphore_signal(barrier, inc=1, device_id=p, device_id_type=MESH)

    br_, bc_ = m_ref.shape
    e1 = (lax.broadcasted_iota(jnp.int32, (rows, br_), 0) // 64
          == lax.broadcasted_iota(jnp.int32, (rows, br_), 1)).astype(jnp.bfloat16)
    e2 = (lax.broadcasted_iota(jnp.int32, (bc_, cols), 1) // 64
          == lax.broadcasted_iota(jnp.int32, (bc_, cols), 0)).astype(jnp.bfloat16)
    rm = jnp.dot(e1, m_ref[...], preferred_element_type=jnp.float32).astype(jnp.bfloat16)
    mask[...] = jnp.dot(rm, e2, preferred_element_type=jnp.float32).astype(jnp.bfloat16)
    tall[0] = t_ref[...] * mask[...]
    pl.semaphore_wait(barrier, len(partners))

    def remote(src, dst, ss, rs, to):
        return pltpu.make_async_remote_copy(
            src_ref=src, dst_ref=dst, send_sem=ss, recv_sem=rs, device_id=to, device_id_type=MESH)

    copies = {}
    sent, got = set(), set()

    def start(key, *args):
        copies[key] = remote(*args)
        copies[key].start()

    def wait_send(key):
        if key not in sent:
            sent.add(key)
            copies[key].wait_send()

    def wait_recv(key):
        if key not in got:
            got.add(key)
            copies[key].wait_recv()

    def own(u):
        rs = pl.ds(u * UN, UN)
        if u >= 2:
            wait_send(("t", 0, u - 2))
            wait_send(("t", 1, u - 2))
        start(("t", 0, u), tall.at[0, rs], tall.at[1, rs], ts.at[0, u], tr.at[0, u], dev(dz=1))
        start(("t", 1, u), tall.at[0, rs], tall.at[2, rs], ts.at[1, u], tr.at[1, u], dev(dz=3))

    def fwd(u):
        rs = pl.ds(u * UN, UN)
        for d in (0, 1):
            wait_recv(("t", d, u))
            if u >= 2:
                wait_send(("t", 2 + d, u - 2))
        start(("t", 2, u), tall.at[1, rs, pl.ds(0, half)], tall.at[3, rs, pl.ds(0, half)],
              ts.at[2, u], tr.at[2, u], dev(dz=1))
        start(("t", 3, u), tall.at[2, rs, pl.ds(half, half)], tall.at[3, rs, pl.ds(half, half)],
              ts.at[3, u], tr.at[3, u], dev(dz=3))

    def arrived(r, j):
        for u in range(j * CH // UN, (j + 1) * CH // UN):
            for d in {0: (), 1: (0,), 2: (1,), 3: (2, 3)}[r]:
                wait_recv(("t", d, u))

    order = [(0, j) for j in range(nj)] + [(r, j) for j in range(nj) for r in (1, 2)] + [(3, j) for j in range(nj)]
    index = {c: i for i, c in enumerate(order)}

    def axes(i):
        if i % 2 == 0:
            return y, ny, lambda d: dev(dy=d), x, nx, lambda d: dev(dx=d)
        return x, nx, lambda d: dev(dx=d), y, ny, lambda d: dev(dy=d)

    def gemm1(q):
        r, j = order[q]
        arrived(r, j)
        p = lax.dot_general(tall[r, j * CH:(j + 1) * CH], mv[...], NT, preferred_element_type=jnp.float32)
        part[q, 0] = p[:, :vh]
        part[q, 1] = p[:, vh:]
        start(("c", q), part.at[q, 1 - h], crecv.at[q], cs.at[q], cr.at[q], dev(flip=True))

    def scatter1(q):
        a, na, to, *_ = axes(q)
        g = CH // na
        wait_recv(("c", q))
        full = part[q, h] + crecv[q]
        s1[q] = full.astype(jnp.bfloat16)
        crecv[q] = full
        for d in range(1, na):
            start(("a", q, d), s1.at[q, pl.ds(pl.multiple_of(lax.rem(a + d, na) * g, g), g)], r1.at[q, d - 1],
                  as_.at[q, d - 1], ar.at[q, d - 1], to(d))

    def scatter2(q):
        a, na, _, b, nb, to = axes(q)
        g = CH // na
        k = g // nb
        total = crecv[q, pl.ds(pl.multiple_of(a * g, g), g)]
        for d in range(1, na):
            wait_recv(("a", q, d))
            total = total + r1[q, d - 1].astype(jnp.float32)
        s2[q] = total
        for d in range(1, nb):
            start(("b", q, d), s2.at[q, pl.ds(pl.multiple_of(lax.rem(b + d, nb) * k, k), k)], r2.at[q, d - 1],
                  bs.at[q, d - 1], br.at[q, d - 1], to(d))

    def piece(q):
        a, na, _, b, nb, _ = axes(q)
        g = CH // na
        k = g // nb
        return pl.ds(pl.multiple_of(a * g + b * k, k), k)

    def finish(q):
        r, j = order[q]
        a, na, _, b, nb, _ = axes(q)
        k = CH // na // nb
        total = s2[q, pl.ds(pl.multiple_of(b * k, k), k)]
        for d in range(1, nb):
            wait_recv(("b", q, d))
            total = total + r2[q, d - 1]
        w = total.astype(jnp.bfloat16)
        if r == 0:
            wg[q, h, piece(q)] = w
            gather1(q)
        else:
            wp[q] = w
            start(("z", q), wp.at[q], wg.at[q, h, piece(q)], zs.at[q], zr.at[q], dev(dz={1: 3, 2: 1, 3: 2}[r]))

    def gather1(q):
        _, _, _, b, nb, to = axes(q)
        if order[q][0] != 0:
            wait_recv(("z", q))
        mine = wg.at[q, h, piece(q)]
        for d in range(1, nb):
            start(("g", q, d), mine, mine, g1s.at[q, d - 1], g1r.at[q, d - 1], to(d))

    def gather2(q):
        a, na, to, _, nb, _ = axes(q)
        g = CH // na
        for d in range(1, nb):
            wait_recv(("g", q, d))
        mine = wg.at[q, h, pl.ds(pl.multiple_of(a * g, g), g)]
        for d in range(1, na):
            start(("h", q, d), mine, mine, g2s.at[q, d - 1], g2r.at[q, d - 1], to(d))

    def gather3(q):
        _, na, *_ = axes(q)
        for d in range(1, na):
            wait_recv(("h", q, d))
        start(("i", q), wg.at[q, h], wg.at[q, h], g3s.at[q], g3r.at[q], dev(flip=True))

    def gemm2(q):
        r, j = order[q]
        slot = {0: 0, 1: 2, 2: 1, 3: 3}[r]
        for jj in range(nj):
            arrived(slot, jj)
        wait_recv(("i", q))
        w = jnp.concatenate([wg[q, 0], wg[q, 1]], axis=1)
        p = jnp.dot(w, tall[slot], preferred_element_type=jnp.float32)
        js = slice(j * CH, (j + 1) * CH)
        if r == 0:
            acc[js] = p
        elif r < 3:
            acc[js] = acc[js] + p
        else:
            out_ref[js] = (acc[js] + p) * mask[js].astype(jnp.float32)

    def prepare():
        mv[...] = v_ref[...] * mask[...]

    events = []

    def at(t, f, *args):
        events.append((t, len(events), f, args))

    unit = 5.3
    for u in range(nu):
        at(max(0.0, unit * (u - 1)), own, u)
        at(unit * nu + 0.5 * unit * (u - 1), fwd, u)
    at(0.1, prepare)
    for q, (r, j) in enumerate(order):
        t = {0: 0.2 + 0.8 * j, 1: 2 * unit * (j + 1) + 1, 2: 2 * unit * (j + 1) + 1.8,
             3: nu * unit + unit * (j + 1) + 2}[r]
        at(t, gemm1, q)
        at(t + 2.6, scatter1, q)
        at(t + 5.6, scatter2, q)
        at(t + 7.6, finish, q)
        if r == 0:
            t -= 2
        else:
            at(t + 9.6, gather1, q)
        at(t + 11.6, gather2, q)
        at(t + 14.6, gather3, q)
        t += 16.2
        if r in (1, 2):
            t = max(t, unit * nu + 3)
        at(t, gemm2, q)
    for _, _, f, args in sorted(events, key=lambda e: e[:2]):
        f(*args)
    for key in copies:
        wait_send(key)


def per_device(t_amp, v_int, block_map, ny, nx):
    rows, cols = t_amp.shape
    nq = 4 * rows // CH
    vh = rows // 2
    k = CH // ny // nx
    bf, f32 = jnp.bfloat16, jnp.float32
    na = max(ny, nx)
    g = CH // min(ny, nx)
    dma = pltpu.SemaphoreType.DMA
    m = jnp.pad(block_map.astype(bf), ((0, 16 - block_map.shape[0]), (0, 128 - block_map.shape[1])))
    vmem = pl.BlockSpec(memory_space=pltpu.VMEM)
    return pl.pallas_call(
        functools.partial(kernel, ny, nx),
        out_shape=jax.ShapeDtypeStruct((rows, cols), f32),
        in_specs=[vmem] * 3,
        out_specs=vmem,
        scratch_shapes=[
            pltpu.VMEM((4, rows, cols), bf),
            pltpu.VMEM((rows, cols), bf),
            pltpu.VMEM((rows, cols), bf),
            pltpu.VMEM((nq, 2, CH, vh), f32),
            pltpu.VMEM((nq, CH, vh), f32),
            pltpu.VMEM((nq, CH, vh), bf),
            pltpu.VMEM((nq, na - 1, g, vh), bf),
            pltpu.VMEM((nq, g, vh), f32),
            pltpu.VMEM((nq, na - 1, k, vh), f32),
            pltpu.VMEM((nq, k, vh), bf),
            pltpu.VMEM((nq, 2, CH, vh), bf),
            pltpu.VMEM((rows, cols), f32),
            dma((4, rows // UN)), dma((4, rows // UN)),
            dma((nq,)), dma((nq,)),
            dma((nq, na - 1)), dma((nq, na - 1)),
            dma((nq, na - 1)), dma((nq, na - 1)),
            dma((nq,)), dma((nq,)),
            dma((nq, na - 1)), dma((nq, na - 1)),
            dma((nq, na - 1)), dma((nq, na - 1)),
            dma((nq,)), dma((nq,)),
        ],
        compiler_params=pltpu.CompilerParams(
            collective_id=0, has_side_effects=True, vmem_limit_bytes=60 * 2**20),
        cost_estimate=pl.CostEstimate(flops=4 * rows * 4 * rows * cols, bytes_accessed=10 * rows * cols, transcendentals=0),
    )(t_amp, v_int, m)


def solution(mesh):
    spec = P("row", ("col", "cuts"))
    body = functools.partial(per_device, ny=mesh.shape["col"] // 2, nx=mesh.shape["cuts"])
    return jax.shard_map(body, mesh=mesh, in_specs=(spec,) * 3, out_specs=spec, check_vma=False)
```

```python
import functools

import jax
import jax.numpy as jnp
from jax import lax
from jax.experimental import pallas as pl
from jax.experimental.pallas import tpu as pltpu
from jax.sharding import PartitionSpec as P

MESH = pl.DeviceIdType.MESH
CH = 256
UN = 128
NP = 4
PACE = 2
LAT = (3.0, 6.0, 4.0, 6.0, 2.0)
NT = (((1,), (1,)), ((), ()))


def kernel(ny, nx, t_ref, v_ref, m_ref, out_ref, tall, mv, mask, part, crecv, s1, r1, wp, wg,
           ts, tr, cs, cr, as_, ar, zs, zr, gs, gr, is_, ir):
    rows, cols = t_ref.shape
    half = cols // 2
    nj = rows // CH
    nu = rows // UN
    vh = rows // 2
    z = lax.axis_index("row")
    col = lax.axis_index("col")
    x = lax.axis_index("cuts")
    y = lax.div(col, 2)
    h = lax.rem(col, 2)

    def dev(dz=0, dy=0, dx=0, flip=False):
        hh = 1 - h if flip else h
        return (lax.rem(z + dz, 4), 2 * lax.rem(y + dy, ny) + hh, lax.rem(x + dx, nx))

    partners = [dev(dz=d) for d in (1, 2, 3)] + [dev(flip=True)]
    partners += [dev(dy=dy, dx=dx) for dy in range(ny) for dx in range(nx) if dy or dx]
    barrier = pltpu.get_barrier_semaphore()
    for p in partners:
        pl.semaphore_signal(barrier, inc=1, device_id=p, device_id_type=MESH)

    br_, bc_ = m_ref.shape
    e1 = (lax.broadcasted_iota(jnp.int32, (rows, br_), 0) // 64
          == lax.broadcasted_iota(jnp.int32, (rows, br_), 1)).astype(jnp.bfloat16)
    e2 = (lax.broadcasted_iota(jnp.int32, (bc_, cols), 1) // 64
          == lax.broadcasted_iota(jnp.int32, (bc_, cols), 0)).astype(jnp.bfloat16)
    rm = jnp.dot(e1, m_ref[...].astype(jnp.bfloat16), preferred_element_type=jnp.float32).astype(jnp.bfloat16)
    mask[...] = jnp.dot(rm, e2, preferred_element_type=jnp.float32).astype(jnp.bfloat16)
    tall[0] = t_ref[...] * mask[...]
    pl.semaphore_wait(barrier, len(partners))

    def remote(src, dst, ss, rs, to):
        return pltpu.make_async_remote_copy(
            src_ref=src, dst_ref=dst, send_sem=ss, recv_sem=rs, device_id=to, device_id_type=MESH)

    copies = {}
    sent, got = set(), set()

    def start(key, *args):
        copies[key] = remote(*args)
        copies[key].start()

    def wait_send(key):
        if key not in sent:
            sent.add(key)
            copies[key].wait_send()

    def wait_recv(key):
        if key not in got:
            got.add(key)
            copies[key].wait_recv()

    def own(u):
        rs = pl.ds(u * UN, UN)
        if u >= PACE:
            wait_send(("t", 0, u - PACE))
            wait_send(("t", 1, u - PACE))
        start(("t", 0, u), tall.at[0, rs], tall.at[1, rs], ts.at[0, u], tr.at[0, u], dev(dz=1))
        start(("t", 1, u), tall.at[0, rs], tall.at[2, rs], ts.at[1, u], tr.at[1, u], dev(dz=3))

    def fwd(u):
        rs = pl.ds(u * UN, UN)
        for d in (0, 1):
            wait_recv(("t", d, u))
            if u >= PACE:
                wait_send(("t", 2 + d, u - PACE))
        start(("t", 2, u), tall.at[1, rs, pl.ds(0, half)], tall.at[3, rs, pl.ds(0, half)],
              ts.at[2, u], tr.at[2, u], dev(dz=1))
        start(("t", 3, u), tall.at[2, rs, pl.ds(half, half)], tall.at[3, rs, pl.ds(half, half)],
              ts.at[3, u], tr.at[3, u], dev(dz=3))

    def arrived(r, j):
        for u in range(j * CH // UN, (j + 1) * CH // UN):
            for d in {0: (), 1: (0,), 2: (1,), 3: (2, 3)}[r]:
                wait_recv(("t", d, u))

    order = [(0, j) for j in range(nj)] + [(r, j) for j in range(nj) for r in (1, 2)] + [(3, j) for j in range(nj)]
    index = {c: i for i, c in enumerate(order)}

    others = [(dy, dx) for dy in range(ny) for dx in range(nx) if dy or dx]
    k = CH // (ny * nx)
    mine = pl.ds(pl.multiple_of((y * nx + x) * k, k), k)
    done = set()

    def gemm1(q):
        r, j = order[q]
        arrived(r, j)
        p = lax.dot_general(tall[r, j * CH:(j + 1) * CH], mv[...], NT, preferred_element_type=jnp.float32)
        if q >= NP:
            assert q - NP in done
            wait_send(("c", q - NP))
        part[q % NP, 0] = p[:, :vh]
        part[q % NP, 1] = p[:, vh:]
        start(("c", q), part.at[q % NP, 1 - h], crecv.at[q], cs.at[q], cr.at[q], dev(flip=True))

    def scatter(q):
        wait_recv(("c", q))
        full = part[q % NP, h] + crecv[q]
        s1[q] = full.astype(jnp.bfloat16)
        crecv[q] = full
        done.add(q)
        for i, (dy, dx) in enumerate(others):
            p = lax.rem(y + dy, ny) * nx + lax.rem(x + dx, nx)
            remote(s1.at[q, pl.ds(pl.multiple_of(p * k, k), k)], r1.at[q, i], as_.at[q], ar.at[q],
                   dev(dy=dy, dx=dx)).start()
        copies[("a", q)] = remote(r1.at[q], r1.at[q], as_.at[q], ar.at[q], dev(dy=1))

    def finish(q):
        r, j = order[q]
        wait_recv(("a", q))
        total = crecv[q, mine]
        for i in range(len(others)):
            total = total + r1[q, i].astype(jnp.float32)
        w = total.astype(jnp.bfloat16)
        if r == 0:
            wg[q, h, mine] = w
            gather1(q)
        else:
            wp[q] = w
            start(("z", q), wp.at[q], wg.at[q, h, mine], zs.at[q], zr.at[q], dev(dz={1: 3, 2: 1, 3: 2}[r]))

    def gather1(q):
        if order[q][0] != 0:
            wait_recv(("z", q))
        src = wg.at[q, h, mine]
        for dy, dx in others:
            remote(src, src, gs.at[q], gr.at[q], dev(dy=dy, dx=dx)).start()
        copies[("g", q)] = remote(r1.at[q], r1.at[q], gs.at[q], gr.at[q], dev(dy=1))

    def gather2(q):
        wait_recv(("g", q))
        start(("i", q), wg.at[q, h], wg.at[q, h], is_.at[q], ir.at[q], dev(flip=True))

    def gemm2(q):
        r, j = order[q]
        slot = {0: 0, 1: 2, 2: 1, 3: 3}[r]
        for jj in range(nj):
            arrived(slot, jj)
        wait_recv(("i", q))
        w = jnp.concatenate([wg[q, 0], wg[q, 1]], axis=1)
        p = jnp.dot(w, tall[slot], preferred_element_type=jnp.float32)
        js = slice(j * CH, (j + 1) * CH)
        if r == 0:
            out_ref[js] = p
        elif r < 3:
            out_ref[js] = out_ref[js] + p
        else:
            out_ref[js] = (out_ref[js] + p) * mask[js].astype(jnp.float32)

    def prepare():
        mv[...] = v_ref[...] * mask[...]

    events = []

    def at(t, f, *args):
        events.append((t, len(events), f, args))

    unit = 5.1
    for u in range(nu):
        at(max(0.0, unit * (u - 1)), own, u)
        at(unit * nu + 0.5 * unit * (u - 1), fwd, u)
    at(0.1, prepare)
    for q, (r, j) in enumerate(order):
        t = {0: 0.2 + 0.8 * j, 1: 2 * unit * (j + 1) + 2, 2: 2 * unit * (j + 1) + 2.8,
             3: nu * unit + unit * (j + 1) + 4}[r]
        at(t, gemm1, q)
        t += LAT[0]
        at(t, scatter, q)
        t += LAT[1]
        at(t, finish, q)
        if r > 0:
            t += LAT[2]
            at(t, gather1, q)
        t += LAT[3]
        at(t, gather2, q)
        t += LAT[4]
        if r in (1, 2):
            t = max(t, unit * nu + 3)
        at(t, gemm2, q)
    for _, _, f, args in sorted(events, key=lambda e: e[:2]):
        f(*args)
    for key in copies:
        wait_send(key)


def per_device(t_amp, v_int, block_map, ny, nx):
    rows, cols = t_amp.shape
    nq = 4 * rows // CH
    vh = rows // 2
    k = CH // ny // nx
    bf, f32 = jnp.bfloat16, jnp.float32
    dma = pltpu.SemaphoreType.DMA
    vmem = pl.BlockSpec(memory_space=pltpu.VMEM)
    return pl.pallas_call(
        functools.partial(kernel, ny, nx),
        out_shape=jax.ShapeDtypeStruct((rows, cols), f32),
        in_specs=[vmem] * 3,
        out_specs=vmem,
        scratch_shapes=[
            pltpu.VMEM((4, rows, cols), bf),
            pltpu.VMEM((rows, cols), bf),
            pltpu.VMEM((rows, cols), bf),
            pltpu.VMEM((NP, 2, CH, vh), f32),
            pltpu.VMEM((nq, CH, vh), f32),
            pltpu.VMEM((nq, CH, vh), bf),
            pltpu.VMEM((nq, ny * nx - 1, k, vh), bf),
            pltpu.VMEM((nq, k, vh), bf),
            pltpu.VMEM((nq, 2, CH, vh), bf),
            dma((4, rows // UN)), dma((4, rows // UN)),
        ] + [dma((nq,))] * 10,
        compiler_params=pltpu.CompilerParams(
            collective_id=0, has_side_effects=True, vmem_limit_bytes=40 * 2**20),
        cost_estimate=pl.CostEstimate(flops=4 * rows * 4 * rows * cols, bytes_accessed=10 * rows * cols, transcendentals=0),
    )(t_amp, v_int, block_map)


def solution(mesh):
    spec = P("row", ("col", "cuts"))
    body = functools.partial(per_device, ny=mesh.shape["col"] // 2, nx=mesh.shape["cuts"])
    return jax.shard_map(body, mesh=mesh, in_specs=(spec,) * 3, out_specs=spec, check_vma=False)
```

```python
import functools

import jax
import jax.numpy as jnp
from jax import lax
from jax.experimental import pallas as pl
from jax.experimental.pallas import tpu as pltpu
from jax.sharding import PartitionSpec as P

MESH = pl.DeviceIdType.MESH
CH = 256
UN = 128
NP = 4
PACE = 99
LAT = (4.5, 7.9, 8.1, 17.2, 5.2)
NT = (((1,), (1,)), ((), ()))


def kernel(ny, nx, t_ref, v_ref, m_ref, out_ref, tall, mv, mask, part, crecv, s1, r1, wp, wg,
           ts, tr, cs, cr, as_, ar, zs, zr, gs, gr, is_, ir):
    rows, cols = t_ref.shape
    half = cols // 2
    nj = rows // CH
    nu = rows // UN
    vh = rows // 2
    z = lax.axis_index("row")
    col = lax.axis_index("col")
    x = lax.axis_index("cuts")
    y = lax.div(col, 2)
    h = lax.rem(col, 2)

    def dev(dz=0, dy=0, dx=0, flip=False):
        hh = 1 - h if flip else h
        return (lax.rem(z + dz, 4), 2 * lax.rem(y + dy, ny) + hh, lax.rem(x + dx, nx))

    partners = [dev(dz=d) for d in (1, 2, 3)] + [dev(flip=True)]
    partners += [dev(dy=dy, dx=dx) for dy in range(ny) for dx in range(nx) if dy or dx]
    barrier = pltpu.get_barrier_semaphore()
    for p in partners:
        pl.semaphore_signal(barrier, inc=1, device_id=p, device_id_type=MESH)

    br_, bc_ = m_ref.shape
    e1 = (lax.broadcasted_iota(jnp.int32, (rows, br_), 0) // 64
          == lax.broadcasted_iota(jnp.int32, (rows, br_), 1)).astype(jnp.bfloat16)
    e2 = (lax.broadcasted_iota(jnp.int32, (bc_, cols), 1) // 64
          == lax.broadcasted_iota(jnp.int32, (bc_, cols), 0)).astype(jnp.bfloat16)
    rm = jnp.dot(e1, m_ref[...].astype(jnp.bfloat16), preferred_element_type=jnp.float32).astype(jnp.bfloat16)
    mask[...] = jnp.dot(rm, e2, preferred_element_type=jnp.float32).astype(jnp.bfloat16)
    tall[0] = t_ref[...] * mask[...]
    pl.semaphore_wait(barrier, len(partners))

    def remote(src, dst, ss, rs, to):
        return pltpu.make_async_remote_copy(
            src_ref=src, dst_ref=dst, send_sem=ss, recv_sem=rs, device_id=to, device_id_type=MESH)

    copies = {}
    sent, got = set(), set()

    def start(key, *args):
        copies[key] = remote(*args)
        copies[key].start()

    def wait_send(key):
        if key not in sent:
            sent.add(key)
            copies[key].wait_send()

    def wait_recv(key):
        if key not in got:
            got.add(key)
            copies[key].wait_recv()

    def own(u):
        rs = pl.ds(u * UN, UN)
        if u >= PACE:
            wait_send(("t", 0, u - PACE))
            wait_send(("t", 1, u - PACE))
        start(("t", 0, u), tall.at[0, rs], tall.at[1, rs], ts.at[0, u], tr.at[0, u], dev(dz=1))
        start(("t", 1, u), tall.at[0, rs], tall.at[2, rs], ts.at[1, u], tr.at[1, u], dev(dz=3))

    def fwd(u):
        rs = pl.ds(u * UN, UN)
        for d in (0, 1):
            wait_recv(("t", d, u))
            if u >= PACE:
                wait_send(("t", 2 + d, u - PACE))
        start(("t", 2, u), tall.at[1, rs, pl.ds(0, half)], tall.at[3, rs, pl.ds(0, half)],
              ts.at[2, u], tr.at[2, u], dev(dz=1))
        start(("t", 3, u), tall.at[2, rs, pl.ds(half, half)], tall.at[3, rs, pl.ds(half, half)],
              ts.at[3, u], tr.at[3, u], dev(dz=3))

    def arrived(r, j):
        for u in range(j * CH // UN, (j + 1) * CH // UN):
            for d in {0: (), 1: (0,), 2: (1,), 3: (2, 3)}[r]:
                wait_recv(("t", d, u))

    order = [(0, j) for j in range(nj)] + [(r, j) for j in range(nj) for r in (1, 2)] + [(3, j) for j in range(nj)]
    index = {c: i for i, c in enumerate(order)}

    others = [(dy, dx) for dy in range(ny) for dx in range(nx) if dy or dx]
    k = CH // (ny * nx)
    mine = pl.ds(pl.multiple_of((y * nx + x) * k, k), k)
    done = set()

    def gemm1(q):
        r, j = order[q]
        arrived(r, j)
        p = lax.dot_general(tall[r, j * CH:(j + 1) * CH], mv[...], NT, preferred_element_type=jnp.float32)
        if q >= NP:
            assert q - NP in done
            wait_send(("c", q - NP))
        part[q % NP, 0] = p[:, :vh]
        part[q % NP, 1] = p[:, vh:]
        start(("c", q), part.at[q % NP, 1 - h], crecv.at[q], cs.at[q], cr.at[q], dev(flip=True))

    def scatter(q):
        wait_recv(("c", q))
        full = part[q % NP, h] + crecv[q]
        s1[q] = full.astype(jnp.bfloat16)
        crecv[q] = full
        done.add(q)
        for i, (dy, dx) in enumerate(others):
            p = lax.rem(y + dy, ny) * nx + lax.rem(x + dx, nx)
            remote(s1.at[q, pl.ds(pl.multiple_of(p * k, k), k)], r1.at[q, i], as_.at[q], ar.at[q],
                   dev(dy=dy, dx=dx)).start()
        copies[("a", q)] = remote(r1.at[q], r1.at[q], as_.at[q], ar.at[q], dev(dy=1))

    def finish(q):
        r, j = order[q]
        wait_recv(("a", q))
        total = crecv[q, mine]
        for i in range(len(others)):
            total = total + r1[q, i].astype(jnp.float32)
        w = total.astype(jnp.bfloat16)
        if r == 0:
            wg[q, h, mine] = w
            gather1(q)
        else:
            wp[q] = w
            start(("z", q), wp.at[q], wg.at[q, h, mine], zs.at[q], zr.at[q], dev(dz={1: 3, 2: 1, 3: 2}[r]))

    def gather1(q):
        if order[q][0] != 0:
            wait_recv(("z", q))
        src = wg.at[q, h, mine]
        for dy, dx in others:
            remote(src, src, gs.at[q], gr.at[q], dev(dy=dy, dx=dx)).start()
        copies[("g", q)] = remote(r1.at[q], r1.at[q], gs.at[q], gr.at[q], dev(dy=1))

    def gather2(q):
        wait_recv(("g", q))
        start(("i", q), wg.at[q, h], wg.at[q, h], is_.at[q], ir.at[q], dev(flip=True))

    def gemm2(q):
        r, j = order[q]
        slot = {0: 0, 1: 2, 2: 1, 3: 3}[r]
        for jj in range(nj):
            arrived(slot, jj)
        wait_recv(("i", q))
        w = jnp.concatenate([wg[q, 0], wg[q, 1]], axis=1)
        p = jnp.dot(w, tall[slot], preferred_element_type=jnp.float32)
        js = slice(j * CH, (j + 1) * CH)
        if r == 0:
            out_ref[js] = p
        elif r < 3:
            out_ref[js] = out_ref[js] + p
        else:
            out_ref[js] = (out_ref[js] + p) * mask[js].astype(jnp.float32)

    def prepare():
        mv[...] = v_ref[...] * mask[...]

    events = []

    def at(t, f, *args):
        events.append((t, len(events), f, args))

    unit = 4.1
    for u in range(nu):
        at(max(0.0, unit * (u - 1)), own, u)
        at(unit * nu + 0.5 * unit * (u - 1), fwd, u)
    at(0.1, prepare)
    for q, (r, j) in enumerate(order):
        t = {0: 0.2 + 0.8 * j, 1: 2 * unit * (j + 1) + 2, 2: 2 * unit * (j + 1) + 2.8,
             3: nu * unit + unit * (j + 1) + 4}[r]
        at(t, gemm1, q)
        t += LAT[0]
        at(t, scatter, q)
        t += LAT[1]
        at(t, finish, q)
        if r > 0:
            t += LAT[2]
            at(t, gather1, q)
        t += LAT[3]
        at(t, gather2, q)
        t += LAT[4]
        if r in (1, 2):
            t = max(t, unit * nu + 3)
        at(t, gemm2, q)
    for _, _, f, args in sorted(events, key=lambda e: e[:2]):
        f(*args)
    for key in copies:
        wait_send(key)


def per_device(t_amp, v_int, block_map, ny, nx):
    rows, cols = t_amp.shape
    nq = 4 * rows // CH
    vh = rows // 2
    k = CH // ny // nx
    bf, f32 = jnp.bfloat16, jnp.float32
    dma = pltpu.SemaphoreType.DMA
    vmem = pl.BlockSpec(memory_space=pltpu.VMEM)
    return pl.pallas_call(
        functools.partial(kernel, ny, nx),
        out_shape=jax.ShapeDtypeStruct((rows, cols), f32),
        in_specs=[vmem] * 3,
        out_specs=vmem,
        scratch_shapes=[
            pltpu.VMEM((4, rows, cols), bf),
            pltpu.VMEM((rows, cols), bf),
            pltpu.VMEM((rows, cols), bf),
            pltpu.VMEM((NP, 2, CH, vh), f32),
            pltpu.VMEM((nq, CH, vh), f32),
            pltpu.VMEM((nq, CH, vh), bf),
            pltpu.VMEM((nq, ny * nx - 1, k, vh), bf),
            pltpu.VMEM((nq, k, vh), bf),
            pltpu.VMEM((nq, 2, CH, vh), bf),
            dma((4, rows // UN)), dma((4, rows // UN)),
        ] + [dma((nq,))] * 10,
        compiler_params=pltpu.CompilerParams(
            collective_id=0, has_side_effects=True, vmem_limit_bytes=40 * 2**20),
        cost_estimate=pl.CostEstimate(flops=4 * rows * 4 * rows * cols, bytes_accessed=10 * rows * cols, transcendentals=0),
    )(t_amp, v_int, block_map)


def solution(mesh):
    spec = P("row", ("col", "cuts"))
    body = functools.partial(per_device, ny=mesh.shape["col"] // 2, nx=mesh.shape["cuts"])
    return jax.shard_map(body, mesh=mesh, in_specs=(spec,) * 3, out_specs=spec, check_vma=False)
```

```python
import functools

import jax
import jax.numpy as jnp
from jax import lax
from jax.experimental import pallas as pl
from jax.experimental.pallas import tpu as pltpu
from jax.sharding import PartitionSpec as P

MESH = pl.DeviceIdType.MESH
CH = 256
UN = 128
NP = 4
LAT = (4.5, 7.9, 8.1, 17.2, 5.2)
NT = (((1,), (1,)), ((), ()))


def kernel(ny, nx, t_ref, v_ref, m_ref, out_ref, tall, mv, mask, part, crecv, s1, r1, wp, wg,
           ms, ls, ts, tr, cs, cr, as_, ar, zs, zr, gs, gr, is_, ir):
    rows, cols = t_ref.shape
    half = cols // 2
    nj = rows // CH
    nu = rows // UN
    vh = rows // 2
    z = lax.axis_index("row")
    col = lax.axis_index("col")
    x = lax.axis_index("cuts")
    y = lax.div(col, 2)
    h = lax.rem(col, 2)

    def dev(dz=0, dy=0, dx=0, flip=False):
        hh = 1 - h if flip else h
        return (lax.rem(z + dz, 4), 2 * lax.rem(y + dy, ny) + hh, lax.rem(x + dx, nx))

    partners = [dev(dz=d) for d in (1, 2, 3)] + [dev(flip=True)]
    partners += [dev(dy=dy, dx=dx) for dy in range(ny) for dx in range(nx) if dy or dx]
    barrier = pltpu.get_barrier_semaphore()
    for p in partners:
        pl.semaphore_signal(barrier, inc=1, device_id=p, device_id_type=MESH)

    units = [pl.ds(u * UN, UN) for u in range(nu)]
    loads = [pltpu.make_async_copy(m_ref, ms, ls.at[0]), pltpu.make_async_copy(v_ref, mv, ls.at[1])]
    loads += [pltpu.make_async_copy(t_ref.at[rs], tall.at[0, rs], ls.at[2 + u]) for u, rs in enumerate(units)]
    for c in [loads[0]] + loads[2:] + [loads[1]]:
        c.start()

    mr, mc = ms.shape
    e1 = (lax.broadcasted_iota(jnp.int32, (rows, mr), 0) // 64
          == lax.broadcasted_iota(jnp.int32, (rows, mr), 1)).astype(jnp.bfloat16)
    e2 = (lax.broadcasted_iota(jnp.int32, (mc, cols), 1) // 64
          == lax.broadcasted_iota(jnp.int32, (mc, cols), 0)).astype(jnp.bfloat16)
    loads[0].wait()
    rm = jnp.dot(e1, ms[...].astype(jnp.bfloat16), preferred_element_type=jnp.float32).astype(jnp.bfloat16)

    def masked(u):
        rs = units[u]
        mask[rs] = jnp.dot(rm[u * UN:(u + 1) * UN], e2, preferred_element_type=jnp.float32).astype(jnp.bfloat16)
        loads[2 + u].wait()
        tall[0, rs] = tall[0, rs] * mask[rs]

    masked(0)
    pl.semaphore_wait(barrier, len(partners))

    def remote(src, dst, ss, rs, to):
        return pltpu.make_async_remote_copy(
            src_ref=src, dst_ref=dst, send_sem=ss, recv_sem=rs, device_id=to, device_id_type=MESH)

    copies = {}
    sent, got = set(), set()

    def start(key, *args):
        copies[key] = remote(*args)
        copies[key].start()

    def wait_send(key):
        if key not in sent:
            sent.add(key)
            copies[key].wait_send()

    def wait_recv(key):
        if key not in got:
            got.add(key)
            copies[key].wait_recv()

    def own(u):
        rs = units[u]
        if u > 0:
            masked(u)
        start(("t", 0, u), tall.at[0, rs], tall.at[1, rs], ts.at[0, u], tr.at[0, u], dev(dz=1))
        start(("t", 1, u), tall.at[0, rs], tall.at[2, rs], ts.at[1, u], tr.at[1, u], dev(dz=3))

    def fwd(u):
        rs = units[u]
        for d in (0, 1):
            wait_recv(("t", d, u))
        start(("t", 2, u), tall.at[1, rs, pl.ds(0, half)], tall.at[3, rs, pl.ds(0, half)],
              ts.at[2, u], tr.at[2, u], dev(dz=1))
        start(("t", 3, u), tall.at[2, rs, pl.ds(half, half)], tall.at[3, rs, pl.ds(half, half)],
              ts.at[3, u], tr.at[3, u], dev(dz=3))

    def arrived(r, j):
        for u in range(j * CH // UN, (j + 1) * CH // UN):
            for d in {0: (), 1: (0,), 2: (1,), 3: (2, 3)}[r]:
                wait_recv(("t", d, u))

    order = [(0, j) for j in range(nj)] + [(r, j) for j in range(nj) for r in (1, 2)] + [(3, j) for j in range(nj)]
    index = {c: i for i, c in enumerate(order)}

    others = [(dy, dx) for dy in (2, 1, 3, 0) for dx in (2, 1, 3, 0) if dy or dx]
    k = CH // (ny * nx)
    mine = pl.ds(pl.multiple_of((y * nx + x) * k, k), k)
    done = set()

    def gemm1(q):
        r, j = order[q]
        arrived(r, j)
        p = lax.dot_general(tall[r, j * CH:(j + 1) * CH], mv[...], NT, preferred_element_type=jnp.float32)
        if q >= NP:
            assert q - NP in done
            wait_send(("c", q - NP))
        part[q % NP, 0] = p[:, :vh]
        part[q % NP, 1] = p[:, vh:]
        start(("c", q), part.at[q % NP, 1 - h], crecv.at[q], cs.at[q], cr.at[q], dev(flip=True))

    def scatter(q):
        wait_recv(("c", q))
        full = part[q % NP, h] + crecv[q]
        s1[q] = full.astype(jnp.bfloat16)
        crecv[q] = full
        done.add(q)
        for i, (dy, dx) in enumerate(others):
            p = lax.rem(y + dy, ny) * nx + lax.rem(x + dx, nx)
            remote(s1.at[q, pl.ds(pl.multiple_of(p * k, k), k)], r1.at[q, i], as_.at[q], ar.at[q],
                   dev(dy=dy, dx=dx)).start()
        copies[("a", q)] = remote(r1.at[q], r1.at[q], as_.at[q], ar.at[q], dev(dy=1))

    def finish(q):
        r, j = order[q]
        wait_recv(("a", q))
        total = crecv[q, mine]
        for i in range(len(others)):
            total = total + r1[q, i].astype(jnp.float32)
        w = total.astype(jnp.bfloat16)
        if r == 0:
            wg[q, h, mine] = w
            gather1(q)
        else:
            wp[q] = w
            start(("z", q), wp.at[q], wg.at[q, h, mine], zs.at[q], zr.at[q], dev(dz={1: 3, 2: 1, 3: 2}[r]))

    def gather1(q):
        if order[q][0] != 0:
            wait_recv(("z", q))
        src = wg.at[q, h, mine]
        for dy, dx in others:
            remote(src, src, gs.at[q], gr.at[q], dev(dy=dy, dx=dx)).start()
        copies[("g", q)] = remote(r1.at[q], r1.at[q], gs.at[q], gr.at[q], dev(dy=1))

    def gather2(q):
        wait_recv(("g", q))
        start(("i", q), wg.at[q, h], wg.at[q, h], is_.at[q], ir.at[q], dev(flip=True))

    def gemm2(q):
        r, j = order[q]
        slot = {0: 0, 1: 2, 2: 1, 3: 3}[r]
        for jj in range(nj):
            arrived(slot, jj)
        wait_recv(("i", q))
        w = jnp.concatenate([wg[q, 0], wg[q, 1]], axis=1)
        p = jnp.dot(w, tall[slot], preferred_element_type=jnp.float32)
        js = slice(j * CH, (j + 1) * CH)
        if r == 0:
            out_ref[js] = p
        elif r < 3:
            out_ref[js] = out_ref[js] + p
        else:
            out_ref[js] = (out_ref[js] + p) * mask[js].astype(jnp.float32)

    def prepare():
        loads[1].wait()
        mv[...] = mv[...] * mask[...]

    events = []

    def at(t, f, *args):
        events.append((t, len(events), f, args))

    unit = 4.1
    for u in range(nu):
        at(0.0, own, u)
        at(unit * nu + 0.5 * unit * (u - 1), fwd, u)
    at(0.1, prepare)
    for q, (r, j) in enumerate(order):
        t = {0: 0.2 + 0.8 * j, 1: 2 * unit * (j + 1) + 2, 2: 2 * unit * (j + 1) + 2.8,
             3: nu * unit + unit * (j + 1) + 4}[r]
        at(t, gemm1, q)
        t += LAT[0]
        at(t, scatter, q)
        t += LAT[1]
        at(t, finish, q)
        if r > 0:
            t += LAT[2]
            at(t, gather1, q)
        t += LAT[3]
        at(t, gather2, q)
        t += LAT[4]
        if r in (1, 2):
            t = max(t, unit * nu + 3)
        at(t, gemm2, q)
    for _, _, f, args in sorted(events, key=lambda e: e[:2]):
        f(*args)
    for key in copies:
        wait_send(key)


def per_device(t_amp, v_int, block_map, ny, nx):
    rows, cols = t_amp.shape
    nq = 4 * rows // CH
    vh = rows // 2
    k = CH // ny // nx
    bf, f32 = jnp.bfloat16, jnp.float32
    dma = pltpu.SemaphoreType.DMA
    vmem = pl.BlockSpec(memory_space=pltpu.VMEM)
    return pl.pallas_call(
        functools.partial(kernel, ny, nx),
        out_shape=jax.ShapeDtypeStruct((rows, cols), f32),
        in_specs=[pl.BlockSpec(memory_space=pltpu.HBM)] * 3,
        out_specs=vmem,
        scratch_shapes=[
            pltpu.VMEM((4, rows, cols), bf),
            pltpu.VMEM((rows, cols), bf),
            pltpu.VMEM((rows, cols), bf),
            pltpu.VMEM((NP, 2, CH, vh), f32),
            pltpu.VMEM((nq, CH, vh), f32),
            pltpu.VMEM((nq, CH, vh), bf),
            pltpu.VMEM((nq, ny * nx - 1, k, vh), bf),
            pltpu.VMEM((nq, k, vh), bf),
            pltpu.VMEM((nq, 2, CH, vh), bf),
            pltpu.VMEM(block_map.shape, jnp.int32),
            dma((2 + rows // UN,)), dma((4, rows // UN)), dma((4, rows // UN)),
        ] + [dma((nq,))] * 10,
        compiler_params=pltpu.CompilerParams(
            collective_id=0, has_side_effects=True, vmem_limit_bytes=40 * 2**20),
        cost_estimate=pl.CostEstimate(flops=4 * rows * 4 * rows * cols, bytes_accessed=10 * rows * cols, transcendentals=0),
    )(*(pltpu.with_memory_space_constraint(a, pltpu.HBM) for a in (t_amp, v_int, block_map)))


def solution(mesh):
    spec = P("row", ("col", "cuts"))
    body = functools.partial(per_device, ny=mesh.shape["col"] // 2, nx=mesh.shape["cuts"])
    return jax.shard_map(body, mesh=mesh, in_specs=(spec,) * 3, out_specs=spec, check_vma=False)
```

```python
import functools

import jax
import jax.numpy as jnp
from jax import lax
from jax.experimental import pallas as pl
from jax.experimental.pallas import tpu as pltpu
from jax.sharding import PartitionSpec as P

MESH = pl.DeviceIdType.MESH
CH = 256
UN = 128
NP = 4
LAT = (3.6, 7.1, 7.5, 20.9, 6.0)
NT = (((1,), (1,)), ((), ()))


def kernel(ny, nx, t_ref, v_ref, m_ref, out_ref, tall, mv, mask, part, crecv, s1, r1, wp, wg,
           ms, ls, ts, tr, cs, cr, as_, ar, zs, zr, gs, gr, is_, ir):
    rows, cols = t_ref.shape
    half = cols // 2
    nj = rows // CH
    nu = rows // UN
    vh = rows // 2
    z = lax.axis_index("row")
    col = lax.axis_index("col")
    x = lax.axis_index("cuts")
    y = lax.div(col, 2)
    h = lax.rem(col, 2)

    def dev(dz=0, dy=0, dx=0, flip=False):
        hh = 1 - h if flip else h
        return (lax.rem(z + dz, 4), 2 * lax.rem(y + dy, ny) + hh, lax.rem(x + dx, nx))

    partners = [dev(dz=d) for d in (1, 2, 3)] + [dev(flip=True)]
    partners += [dev(dy=dy, dx=dx) for dy in range(ny) for dx in range(nx) if dy or dx]
    barrier = pltpu.get_barrier_semaphore()
    for p in partners:
        pl.semaphore_signal(barrier, inc=1, device_id=p, device_id_type=MESH)

    units = [pl.ds(u * UN, UN) for u in range(nu)]
    loads = [pltpu.make_async_copy(m_ref, ms, ls.at[0]), pltpu.make_async_copy(v_ref, mv, ls.at[1])]
    loads += [pltpu.make_async_copy(t_ref.at[rs], tall.at[0, rs], ls.at[2 + u]) for u, rs in enumerate(units)]
    for c in [loads[0]] + loads[2:] + [loads[1]]:
        c.start()

    mr, mc = ms.shape
    e1 = (lax.broadcasted_iota(jnp.int32, (rows, mr), 0) // 64
          == lax.broadcasted_iota(jnp.int32, (rows, mr), 1)).astype(jnp.bfloat16)
    e2 = (lax.broadcasted_iota(jnp.int32, (mc, cols), 1) // 64
          == lax.broadcasted_iota(jnp.int32, (mc, cols), 0)).astype(jnp.bfloat16)
    loads[0].wait()
    rm = jnp.dot(e1, ms[...].astype(jnp.bfloat16), preferred_element_type=jnp.float32).astype(jnp.bfloat16)

    def masked(u):
        rs = units[u]
        mask[rs] = jnp.dot(rm[u * UN:(u + 1) * UN], e2, preferred_element_type=jnp.float32).astype(jnp.bfloat16)
        loads[2 + u].wait()
        tall[0, rs] = tall[0, rs] * mask[rs]

    masked(0)
    pl.semaphore_wait(barrier, len(partners))

    def remote(src, dst, ss, rs, to):
        return pltpu.make_async_remote_copy(
            src_ref=src, dst_ref=dst, send_sem=ss, recv_sem=rs, device_id=to, device_id_type=MESH)

    copies = {}
    sent, got = set(), set()

    def start(key, *args):
        copies[key] = remote(*args)
        copies[key].start()

    def wait_send(key):
        if key not in sent:
            sent.add(key)
            copies[key].wait_send()

    def wait_recv(key):
        if key not in got:
            got.add(key)
            copies[key].wait_recv()

    def own(u):
        rs = units[u]
        if u > 0:
            masked(u)
        start(("t", 0, u), tall.at[0, rs], tall.at[1, rs], ts.at[0, u], tr.at[0, u], dev(dz=1))
        start(("t", 1, u), tall.at[0, rs], tall.at[2, rs], ts.at[1, u], tr.at[1, u], dev(dz=3))

    def fwd(u):
        rs = units[u]
        for d in (0, 1):
            wait_recv(("t", d, u))
        start(("t", 2, u), tall.at[1, rs, pl.ds(0, half)], tall.at[3, rs, pl.ds(0, half)],
              ts.at[2, u], tr.at[2, u], dev(dz=1))
        start(("t", 3, u), tall.at[2, rs, pl.ds(half, half)], tall.at[3, rs, pl.ds(half, half)],
              ts.at[3, u], tr.at[3, u], dev(dz=3))

    def arrived(r, j):
        for u in range(j * CH // UN, (j + 1) * CH // UN):
            for d in {0: (), 1: (0,), 2: (1,), 3: (2, 3)}[r]:
                wait_recv(("t", d, u))

    order = [(0, j) for j in range(nj)] + [(r, j) for j in range(nj) for r in (1, 2)] + [(3, j) for j in range(nj)]
    index = {c: i for i, c in enumerate(order)}

    others = [(dy, dx) for dy in (2, 1, 3, 0) for dx in (2, 1, 3, 0) if dy or dx]
    k = CH // (ny * nx)
    mine = pl.ds(pl.multiple_of((y * nx + x) * k, k), k)
    done = set()

    def gemm1(q):
        r, j = order[q]
        arrived(r, j)
        p = lax.dot_general(tall[r, j * CH:(j + 1) * CH], mv[...], NT, preferred_element_type=jnp.float32)
        if q >= NP:
            assert q - NP in done
            wait_send(("c", q - NP))
        part[q % NP, 0] = p[:, :vh]
        part[q % NP, 1] = p[:, vh:]
        start(("c", q), part.at[q % NP, 1 - h], crecv.at[q], cs.at[q], cr.at[q], dev(flip=True))

    last = len(order) - 1

    def gemm1_unit(i):
        r, j = order[last]
        u = j * CH // UN + i
        for d in (2, 3):
            wait_recv(("t", d, u))
        if i == 0:
            assert last - NP in done
            wait_send(("c", last - NP))
        p = lax.dot_general(tall[r, u * UN:(u + 1) * UN], mv[...], NT, preferred_element_type=jnp.float32)
        at_ = pl.ds(i * UN, UN)
        part[last % NP, 0, at_] = p[:, :vh]
        part[last % NP, 1, at_] = p[:, vh:]
        start(("c", last + i), part.at[last % NP, 1 - h, at_], crecv.at[last, at_], cs.at[last + i],
              cr.at[last + i], dev(flip=True))

    def scatter(q):
        for i in range(CH // UN if q == last else 1):
            wait_recv(("c", q + i))
        full = part[q % NP, h] + crecv[q]
        s1[q] = full.astype(jnp.bfloat16)
        crecv[q] = full
        done.add(q)
        for i, (dy, dx) in enumerate(others):
            p = lax.rem(y + dy, ny) * nx + lax.rem(x + dx, nx)
            remote(s1.at[q, pl.ds(pl.multiple_of(p * k, k), k)], r1.at[q, i], as_.at[q], ar.at[q],
                   dev(dy=dy, dx=dx)).start()
        copies[("a", q)] = remote(r1.at[q], r1.at[q], as_.at[q], ar.at[q], dev(dy=1))

    def finish(q):
        r, j = order[q]
        wait_recv(("a", q))
        total = crecv[q, mine]
        for i in range(len(others)):
            total = total + r1[q, i].astype(jnp.float32)
        w = total.astype(jnp.bfloat16)
        if r == 0:
            wg[q, h, mine] = w
            gather1(q)
        else:
            wp[q] = w
            start(("z", q), wp.at[q], wg.at[q, h, mine], zs.at[q], zr.at[q], dev(dz={1: 3, 2: 1, 3: 2}[r]))

    def gather1(q):
        if order[q][0] != 0:
            wait_recv(("z", q))
        src = wg.at[q, h, mine]
        for dy, dx in others:
            remote(src, src, gs.at[q], gr.at[q], dev(dy=dy, dx=dx)).start()
        copies[("g", q)] = remote(r1.at[q], r1.at[q], gs.at[q], gr.at[q], dev(dy=1))

    def gather2(q):
        wait_recv(("g", q))
        start(("i", q), wg.at[q, h], wg.at[q, h], is_.at[q], ir.at[q], dev(flip=True))

    def gemm2(q):
        r, j = order[q]
        slot = {0: 0, 1: 2, 2: 1, 3: 3}[r]
        for jj in range(nj):
            arrived(slot, jj)
        wait_recv(("i", q))
        w = jnp.concatenate([wg[q, 0], wg[q, 1]], axis=1)
        p = jnp.dot(w, tall[slot], preferred_element_type=jnp.float32)
        js = slice(j * CH, (j + 1) * CH)
        if r == 0:
            out_ref[js] = p
        elif r < 3:
            out_ref[js] = out_ref[js] + p
        else:
            out_ref[js] = (out_ref[js] + p) * mask[js].astype(jnp.float32)

    def gemm2_part(own_half):
        r, j = order[last]
        js = slice(j * CH, (j + 1) * CH)
        side = h if own_half else 1 - h
        if not own_half:
            wait_recv(("i", last))
        p = jnp.dot(wg[last, side], tall[r, pl.ds(pl.multiple_of(side * vh, vh), vh)],
                    preferred_element_type=jnp.float32)
        total = out_ref[js] + p
        out_ref[js] = total if own_half else total * mask[js].astype(jnp.float32)

    def prepare():
        loads[1].wait()
        mv[...] = mv[...] * mask[...]

    events = []

    def at(t, f, *args):
        events.append((t, len(events), f, args))

    unit = 3.9
    for u in range(nu):
        at(0.0, own, u)
        at(unit * nu + 0.5 * unit * (u - 1), fwd, u)
    at(0.1, prepare)
    for q, (r, j) in enumerate(order):
        t = {0: 0.2 + 0.8 * j, 1: 2 * unit * (j + 1) + 2, 2: 2 * unit * (j + 1) + 2.8,
             3: nu * unit + unit * (j + 1) + 4}[r]
        if q == last:
            at(t, gemm1_unit, 0)
            at(t, gemm1_unit, 1)
        else:
            at(t, gemm1, q)
        t += LAT[0]
        at(t, scatter, q)
        t += LAT[1]
        at(t, finish, q)
        if r > 0:
            t += LAT[2]
            at(t, gather1, q)
        t += LAT[3]
        at(t, gather2, q)
        if q == last:
            at(t, gemm2_part, True)
        t += LAT[4]
        if r in (1, 2):
            t = max(t, unit * nu + 3)
        if q == last:
            at(t, gemm2_part, False)
        else:
            at(t, gemm2, q)
    for _, _, f, args in sorted(events, key=lambda e: e[:2]):
        f(*args)
    for key in copies:
        wait_send(key)


def per_device(t_amp, v_int, block_map, ny, nx):
    rows, cols = t_amp.shape
    nq = 4 * rows // CH
    vh = rows // 2
    k = CH // ny // nx
    bf, f32 = jnp.bfloat16, jnp.float32
    dma = pltpu.SemaphoreType.DMA
    vmem = pl.BlockSpec(memory_space=pltpu.VMEM)
    return pl.pallas_call(
        functools.partial(kernel, ny, nx),
        out_shape=jax.ShapeDtypeStruct((rows, cols), f32),
        in_specs=[pl.BlockSpec(memory_space=pltpu.HBM)] * 3,
        out_specs=vmem,
        scratch_shapes=[
            pltpu.VMEM((4, rows, cols), bf),
            pltpu.VMEM((rows, cols), bf),
            pltpu.VMEM((rows, cols), bf),
            pltpu.VMEM((NP, 2, CH, vh), f32),
            pltpu.VMEM((nq, CH, vh), f32),
            pltpu.VMEM((nq, CH, vh), bf),
            pltpu.VMEM((nq, ny * nx - 1, k, vh), bf),
            pltpu.VMEM((nq, k, vh), bf),
            pltpu.VMEM((nq, 2, CH, vh), bf),
            pltpu.VMEM(block_map.shape, jnp.int32),
            dma((2 + rows // UN,)), dma((4, rows // UN)), dma((4, rows // UN)),
        ] + [dma((nq + CH // UN - 1,))] * 2 + [dma((nq,))] * 8,
        compiler_params=pltpu.CompilerParams(
            collective_id=0, has_side_effects=True, vmem_limit_bytes=40 * 2**20),
        cost_estimate=pl.CostEstimate(flops=4 * rows * 4 * rows * cols, bytes_accessed=10 * rows * cols, transcendentals=0),
    )(*(pltpu.with_memory_space_constraint(a, pltpu.HBM) for a in (t_amp, v_int, block_map)))


def solution(mesh):
    spec = P("row", ("col", "cuts"))
    body = functools.partial(per_device, ny=mesh.shape["col"] // 2, nx=mesh.shape["cuts"])
    return jax.shard_map(body, mesh=mesh, in_specs=(spec,) * 3, out_specs=spec, check_vma=False)
```

```python
import functools

import jax
import jax.numpy as jnp
from jax import lax
from jax.experimental import pallas as pl
from jax.experimental.pallas import tpu as pltpu
from jax.sharding import PartitionSpec as P

MESH = pl.DeviceIdType.MESH
CH = 256
UN = 128
NP = 4
LAT = (3.6, 7.1, 7.5, 20.9, 6.0)
NT = (((1,), (1,)), ((), ()))


def kernel(ny, nx, t_ref, v_ref, m_ref, out_ref, tall, mv, mask, part, crecv, s1, r1, wp, wg,
           ms, ls, ts, tr, cs, cr, as_, ar, zs, zr, gs, gr, is_, ir):
    rows, cols = t_ref.shape
    half = cols // 2
    nj = rows // CH
    nu = rows // UN
    vh = rows // 2
    z = lax.axis_index("row")
    col = lax.axis_index("col")
    x = lax.axis_index("cuts")
    y = lax.div(col, 2)
    h = lax.rem(col, 2)

    def dev(dz=0, dy=0, dx=0, flip=False):
        hh = 1 - h if flip else h
        return (lax.rem(z + dz, 4), 2 * lax.rem(y + dy, ny) + hh, lax.rem(x + dx, nx))

    partners = [dev(dz=d) for d in (1, 2, 3)] + [dev(flip=True)]
    partners += [dev(dy=dy, dx=dx) for dy in range(ny) for dx in range(nx) if dy or dx]
    barrier = pltpu.get_barrier_semaphore()
    for p in partners:
        pl.semaphore_signal(barrier, inc=1, device_id=p, device_id_type=MESH)

    units = [pl.ds(u * UN, UN) for u in range(nu)]
    loads = [pltpu.make_async_copy(m_ref, ms, ls.at[0]), pltpu.make_async_copy(v_ref, mv, ls.at[1])]
    loads += [pltpu.make_async_copy(t_ref.at[rs], tall.at[0, rs], ls.at[2 + u]) for u, rs in enumerate(units)]
    for c in [loads[0]] + loads[2:] + [loads[1]]:
        c.start()

    mr, mc = ms.shape
    e1 = (lax.broadcasted_iota(jnp.int32, (rows, mr), 0) // 64
          == lax.broadcasted_iota(jnp.int32, (rows, mr), 1)).astype(jnp.bfloat16)
    e2 = (lax.broadcasted_iota(jnp.int32, (mc, cols), 1) // 64
          == lax.broadcasted_iota(jnp.int32, (mc, cols), 0)).astype(jnp.bfloat16)
    loads[0].wait()
    rm = jnp.dot(e1, ms[...].astype(jnp.bfloat16), preferred_element_type=jnp.float32).astype(jnp.bfloat16)

    def masked(u):
        rs = units[u]
        mask[rs] = jnp.dot(rm[u * UN:(u + 1) * UN], e2, preferred_element_type=jnp.float32).astype(jnp.bfloat16)
        loads[2 + u].wait()
        tall[0, rs] = tall[0, rs] * mask[rs]

    masked(0)
    pl.semaphore_wait(barrier, len(partners))

    def remote(src, dst, ss, rs, to):
        return pltpu.make_async_remote_copy(
            src_ref=src, dst_ref=dst, send_sem=ss, recv_sem=rs, device_id=to, device_id_type=MESH)

    copies = {}
    sent, got = set(), set()

    def start(key, *args):
        copies[key] = remote(*args)
        copies[key].start()

    def wait_send(key):
        if key not in sent:
            sent.add(key)
            copies[key].wait_send()

    def wait_recv(key):
        if key not in got:
            got.add(key)
            copies[key].wait_recv()

    def own(u):
        rs = units[u]
        if u > 0:
            masked(u)
        start(("t", 0, u), tall.at[0, rs], tall.at[1, rs], ts.at[0, u], tr.at[0, u], dev(dz=1))
        start(("t", 1, u), tall.at[0, rs], tall.at[2, rs], ts.at[1, u], tr.at[1, u], dev(dz=3))

    def fwd(u):
        rs = units[u]
        for d in (0, 1):
            wait_recv(("t", d, u))
        start(("t", 2, u), tall.at[1, rs, pl.ds(0, half)], tall.at[3, rs, pl.ds(0, half)],
              ts.at[2, u], tr.at[2, u], dev(dz=1))
        start(("t", 3, u), tall.at[2, rs, pl.ds(half, half)], tall.at[3, rs, pl.ds(half, half)],
              ts.at[3, u], tr.at[3, u], dev(dz=3))

    def arrived(r, j):
        for u in range(j * CH // UN, (j + 1) * CH // UN):
            for d in {0: (), 1: (0,), 2: (1,), 3: (2, 3)}[r]:
                wait_recv(("t", d, u))

    order = [(0, j) for j in range(nj)] + [(r, j) for j in range(nj) for r in (1, 2)] + [(3, j) for j in range(nj)]
    index = {c: i for i, c in enumerate(order)}

    others = [(dy, dx) for dy in (0, 1, 3, 2) for dx in (0, 1, 3, 2) if dy or dx]
    k = CH // (ny * nx)
    mine = pl.ds(pl.multiple_of((y * nx + x) * k, k), k)
    done = set()

    def gemm1(q):
        r, j = order[q]
        arrived(r, j)
        p = lax.dot_general(tall[r, j * CH:(j + 1) * CH], mv[...], NT, preferred_element_type=jnp.float32)
        if q >= NP:
            assert q - NP in done
            wait_send(("c", q - NP))
        part[q % NP, 0] = p[:, :vh]
        part[q % NP, 1] = p[:, vh:]
        start(("c", q), part.at[q % NP, 1 - h], crecv.at[q], cs.at[q], cr.at[q], dev(flip=True))

    last = len(order) - 1

    def gemm1_unit(i):
        r, j = order[last]
        u = j * CH // UN + i
        for d in (2, 3):
            wait_recv(("t", d, u))
        if i == 0:
            assert last - NP in done
            wait_send(("c", last - NP))
        p = lax.dot_general(tall[r, u * UN:(u + 1) * UN], mv[...], NT, preferred_element_type=jnp.float32)
        at_ = pl.ds(i * UN, UN)
        part[last % NP, 0, at_] = p[:, :vh]
        part[last % NP, 1, at_] = p[:, vh:]
        start(("c", last + i), part.at[last % NP, 1 - h, at_], crecv.at[last, at_], cs.at[last + i],
              cr.at[last + i], dev(flip=True))

    def scatter(q):
        for i in range(CH // UN if q == last else 1):
            wait_recv(("c", q + i))
        full = part[q % NP, h] + crecv[q]
        s1[q] = full.astype(jnp.bfloat16)
        crecv[q] = full
        done.add(q)
        for i, (dy, dx) in enumerate(others):
            p = lax.rem(y + dy, ny) * nx + lax.rem(x + dx, nx)
            remote(s1.at[q, pl.ds(pl.multiple_of(p * k, k), k)], r1.at[q, i], as_.at[q], ar.at[q],
                   dev(dy=dy, dx=dx)).start()
        copies[("a", q)] = remote(r1.at[q], r1.at[q], as_.at[q], ar.at[q], dev(dy=1))

    def finish(q):
        r, j = order[q]
        wait_recv(("a", q))
        total = crecv[q, mine]
        for i in range(len(others)):
            total = total + r1[q, i].astype(jnp.float32)
        w = total.astype(jnp.bfloat16)
        if r == 0:
            wg[q, h, mine] = w
            gather1(q)
        else:
            wp[q] = w
            start(("z", q), wp.at[q], wg.at[q, h, mine], zs.at[q], zr.at[q], dev(dz={1: 3, 2: 1, 3: 2}[r]))

    def gather1(q):
        if order[q][0] != 0:
            wait_recv(("z", q))
        src = wg.at[q, h, mine]
        for dy, dx in others:
            remote(src, src, gs.at[q], gr.at[q], dev(dy=dy, dx=dx)).start()
        copies[("g", q)] = remote(r1.at[q], r1.at[q], gs.at[q], gr.at[q], dev(dy=1))

    def gather2(q):
        wait_recv(("g", q))
        start(("i", q), wg.at[q, h], wg.at[q, h], is_.at[q], ir.at[q], dev(flip=True))

    def gemm2(q):
        r, j = order[q]
        slot = {0: 0, 1: 2, 2: 1, 3: 3}[r]
        for jj in range(nj):
            arrived(slot, jj)
        wait_recv(("i", q))
        w = jnp.concatenate([wg[q, 0], wg[q, 1]], axis=1)
        p = jnp.dot(w, tall[slot], preferred_element_type=jnp.float32)
        js = slice(j * CH, (j + 1) * CH)
        if r == 0:
            out_ref[js] = p
        elif r < 3:
            out_ref[js] = out_ref[js] + p
        else:
            out_ref[js] = (out_ref[js] + p) * mask[js].astype(jnp.float32)

    def gemm2_part(own_half):
        r, j = order[last]
        js = slice(j * CH, (j + 1) * CH)
        side = h if own_half else 1 - h
        if not own_half:
            wait_recv(("i", last))
        p = jnp.dot(wg[last, side], tall[r, pl.ds(pl.multiple_of(side * vh, vh), vh)],
                    preferred_element_type=jnp.float32)
        total = out_ref[js] + p
        out_ref[js] = total if own_half else total * mask[js].astype(jnp.float32)

    def drain(q):
        for key in list(copies):
            if key[0] == "t" or key[1] <= q:
                wait_send(key)

    def prepare():
        loads[1].wait()
        mv[...] = mv[...] * mask[...]

    events = []

    def at(t, f, *args):
        events.append((t, len(events), f, args))

    unit = 3.9
    for u in range(nu):
        at(0.0, own, u)
        at(unit * nu + 0.5 * unit * (u - 1), fwd, u)
    at(0.1, prepare)
    for q, (r, j) in enumerate(order):
        t = {0: 0.2 + 0.8 * j, 1: 2 * unit * (j + 1) + 2, 2: 2 * unit * (j + 1) + 2.8,
             3: nu * unit + unit * (j + 1) + 4}[r]
        if q == last:
            at(t, gemm1_unit, 0)
            at(t, gemm1_unit, 1)
        else:
            at(t, gemm1, q)
        t += LAT[0]
        at(t, scatter, q)
        if q == last:
            at(t, drain, last - 3)
        t += LAT[1]
        at(t, finish, q)
        if r > 0:
            t += LAT[2]
            if q == last:
                at(t, drain, last - 2)
            at(t, gather1, q)
        t += LAT[3]
        at(t, gather2, q)
        if q == last:
            at(t, gemm2_part, True)
        t += LAT[4]
        if r in (1, 2):
            t = max(t, unit * nu + 3)
        if q == last:
            at(t, drain, last - 1)
            at(t, gemm2_part, False)
        else:
            at(t, gemm2, q)
    for _, _, f, args in sorted(events, key=lambda e: e[:2]):
        f(*args)
    for key in copies:
        wait_send(key)


def per_device(t_amp, v_int, block_map, ny, nx):
    rows, cols = t_amp.shape
    nq = 4 * rows // CH
    vh = rows // 2
    k = CH // ny // nx
    bf, f32 = jnp.bfloat16, jnp.float32
    dma = pltpu.SemaphoreType.DMA
    vmem = pl.BlockSpec(memory_space=pltpu.VMEM)
    return pl.pallas_call(
        functools.partial(kernel, ny, nx),
        out_shape=jax.ShapeDtypeStruct((rows, cols), f32),
        in_specs=[pl.BlockSpec(memory_space=pltpu.HBM)] * 3,
        out_specs=vmem,
        scratch_shapes=[
            pltpu.VMEM((4, rows, cols), bf),
            pltpu.VMEM((rows, cols), bf),
            pltpu.VMEM((rows, cols), bf),
            pltpu.VMEM((NP, 2, CH, vh), f32),
            pltpu.VMEM((nq, CH, vh), f32),
            pltpu.VMEM((nq, CH, vh), bf),
            pltpu.VMEM((nq, ny * nx - 1, k, vh), bf),
            pltpu.VMEM((nq, k, vh), bf),
            pltpu.VMEM((nq, 2, CH, vh), bf),
            pltpu.VMEM(block_map.shape, jnp.int32),
            dma((2 + rows // UN,)), dma((4, rows // UN)), dma((4, rows // UN)),
        ] + [dma((nq + CH // UN - 1,))] * 2 + [dma((nq,))] * 8,
        compiler_params=pltpu.CompilerParams(
            collective_id=0, has_side_effects=True, vmem_limit_bytes=40 * 2**20),
        cost_estimate=pl.CostEstimate(flops=4 * rows * 4 * rows * cols, bytes_accessed=10 * rows * cols, transcendentals=0),
    )(*(pltpu.with_memory_space_constraint(a, pltpu.HBM) for a in (t_amp, v_int, block_map)))


def solution(mesh):
    spec = P("row", ("col", "cuts"))
    body = functools.partial(per_device, ny=mesh.shape["col"] // 2, nx=mesh.shape["cuts"])
    return jax.shard_map(body, mesh=mesh, in_specs=(spec,) * 3, out_specs=spec, check_vma=False)
```

```python
import functools

import jax
import jax.numpy as jnp
from jax import lax
from jax.experimental import pallas as pl
from jax.experimental.pallas import tpu as pltpu
from jax.sharding import PartitionSpec as P

MESH = pl.DeviceIdType.MESH
CH = 256
UN = 128
NP = 4
LAT = (3.6, 7.1, 7.5, 20.9, 6.0)
NT = (((1,), (1,)), ((), ()))


def kernel(ny, nx, t_ref, v_ref, m_ref, out_ref, tall, mv, mask, part, crecv, s1, r1, wp, wg,
           ms, ls, ts, tr, cs, cr, as_, ar, zs, zr, gs, gr, is_, ir):
    rows, cols = t_ref.shape
    half = cols // 2
    nj = rows // CH
    nu = rows // UN
    vh = rows // 2
    z = lax.axis_index("row")
    col = lax.axis_index("col")
    x = lax.axis_index("cuts")
    y = lax.div(col, 2)
    h = lax.rem(col, 2)

    def dev(dz=0, dy=0, dx=0, flip=False):
        hh = 1 - h if flip else h
        return (lax.rem(z + dz, 4), 2 * lax.rem(y + dy, ny) + hh, lax.rem(x + dx, nx))

    partners = [dev(dz=d) for d in (1, 2, 3)] + [dev(flip=True)]
    partners += [dev(dy=dy, dx=dx) for dy in range(ny) for dx in range(nx) if dy or dx]
    barrier = pltpu.get_barrier_semaphore()
    for p in partners:
        pl.semaphore_signal(barrier, inc=1, device_id=p, device_id_type=MESH)

    units = [pl.ds(u * UN, UN) for u in range(nu)]
    loads = [pltpu.make_async_copy(m_ref, ms, ls.at[0]), pltpu.make_async_copy(v_ref, mv, ls.at[1])]
    loads += [pltpu.make_async_copy(t_ref.at[rs], tall.at[0, rs], ls.at[2 + u]) for u, rs in enumerate(units)]
    for c in [loads[0]] + loads[2:] + [loads[1]]:
        c.start()

    mr, mc = ms.shape
    e1 = (lax.broadcasted_iota(jnp.int32, (rows, mr), 0) // 64
          == lax.broadcasted_iota(jnp.int32, (rows, mr), 1)).astype(jnp.bfloat16)
    e2 = (lax.broadcasted_iota(jnp.int32, (mc, cols), 1) // 64
          == lax.broadcasted_iota(jnp.int32, (mc, cols), 0)).astype(jnp.bfloat16)
    loads[0].wait()
    rm = jnp.dot(e1, ms[...].astype(jnp.bfloat16), preferred_element_type=jnp.float32).astype(jnp.bfloat16)

    def masked(u):
        rs = units[u]
        mask[rs] = jnp.dot(rm[u * UN:(u + 1) * UN], e2, preferred_element_type=jnp.float32).astype(jnp.bfloat16)
        loads[2 + u].wait()
        tall[0, rs] = tall[0, rs] * mask[rs]

    masked(0)
    pl.semaphore_wait(barrier, len(partners))

    def remote(src, dst, ss, rs, to):
        return pltpu.make_async_remote_copy(
            src_ref=src, dst_ref=dst, send_sem=ss, recv_sem=rs, device_id=to, device_id_type=MESH)

    copies = {}
    sent, got = set(), set()

    def start(key, *args):
        copies[key] = remote(*args)
        copies[key].start()

    def wait_send(key):
        if key not in sent:
            sent.add(key)
            copies[key].wait_send()

    def wait_recv(key):
        if key not in got:
            got.add(key)
            copies[key].wait_recv()

    def own(u):
        rs = units[u]
        if u > 0:
            masked(u)
        start(("t", 0, u), tall.at[0, rs], tall.at[1, rs], ts.at[0, u], tr.at[0, u], dev(dz=1))
        start(("t", 1, u), tall.at[0, rs], tall.at[2, rs], ts.at[1, u], tr.at[1, u], dev(dz=3))

    def fwd(u):
        rs = units[u]
        for d in (0, 1):
            wait_recv(("t", d, u))
        start(("t", 2, u), tall.at[1, rs, pl.ds(0, half)], tall.at[3, rs, pl.ds(0, half)],
              ts.at[2, u], tr.at[2, u], dev(dz=1))
        start(("t", 3, u), tall.at[2, rs, pl.ds(half, half)], tall.at[3, rs, pl.ds(half, half)],
              ts.at[3, u], tr.at[3, u], dev(dz=3))

    def arrived(r, j):
        for u in range(j * CH // UN, (j + 1) * CH // UN):
            for d in {0: (), 1: (0,), 2: (1,), 3: (2, 3)}[r]:
                wait_recv(("t", d, u))

    order = [(0, j) for j in range(nj)] + [(r, j) for j in range(nj) for r in (1, 2)] + [(3, j) for j in range(nj)]
    index = {c: i for i, c in enumerate(order)}

    others = [(dy, dx) for dy in (2, 1, 3, 0) for dx in (2, 1, 3, 0) if dy or dx]
    k = CH // (ny * nx)
    mine = pl.ds(pl.multiple_of((y * nx + x) * k, k), k)
    done = set()

    def gemm1(q):
        r, j = order[q]
        arrived(r, j)
        p = lax.dot_general(tall[r, j * CH:(j + 1) * CH], mv[...], NT, preferred_element_type=jnp.float32)
        if q >= NP:
            assert q - NP in done
            wait_send(("c", q - NP))
        part[q % NP, 0] = p[:, :vh]
        part[q % NP, 1] = p[:, vh:]
        start(("c", q), part.at[q % NP, 1 - h], crecv.at[q], cs.at[q], cr.at[q], dev(flip=True))

    last = len(order) - 1

    def gemm1_unit(i):
        r, j = order[last]
        u = j * CH // UN + i
        for d in (2, 3):
            wait_recv(("t", d, u))
        if i == 0:
            assert last - NP in done
            wait_send(("c", last - NP))
        p = lax.dot_general(tall[r, u * UN:(u + 1) * UN], mv[...], NT, preferred_element_type=jnp.float32)
        at_ = pl.ds(i * UN, UN)
        part[last % NP, 0, at_] = p[:, :vh]
        part[last % NP, 1, at_] = p[:, vh:]
        start(("c", last + i), part.at[last % NP, 1 - h, at_], crecv.at[last, at_], cs.at[last + i],
              cr.at[last + i], dev(flip=True))

    def scatter(q):
        for i in range(CH // UN if q == last else 1):
            wait_recv(("c", q + i))
        full = part[q % NP, h] + crecv[q]
        s1[q] = full.astype(jnp.bfloat16)
        crecv[q] = full
        done.add(q)
        for i, (dy, dx) in enumerate(others):
            p = lax.rem(y + dy, ny) * nx + lax.rem(x + dx, nx)
            remote(s1.at[q, pl.ds(pl.multiple_of(p * k, k), k)], r1.at[q, i], as_.at[q], ar.at[q],
                   dev(dy=dy, dx=dx)).start()
        copies[("a", q)] = remote(r1.at[q], r1.at[q], as_.at[q], ar.at[q], dev(dy=1))

    def finish(q):
        r, j = order[q]
        wait_recv(("a", q))
        total = crecv[q, mine]
        for i in range(len(others)):
            total = total + r1[q, i].astype(jnp.float32)
        w = total.astype(jnp.bfloat16)
        if r == 0:
            wg[q, h, mine] = w
            gather1(q)
        else:
            wp[q] = w
            start(("z", q), wp.at[q], wg.at[q, h, mine], zs.at[q], zr.at[q], dev(dz={1: 3, 2: 1, 3: 2}[r]))

    def gather1(q):
        if order[q][0] != 0:
            wait_recv(("z", q))
        src = wg.at[q, h, mine]
        for dy, dx in others:
            remote(src, src, gs.at[q], gr.at[q], dev(dy=dy, dx=dx)).start()
        copies[("g", q)] = remote(r1.at[q], r1.at[q], gs.at[q], gr.at[q], dev(dy=1))

    def gather2(q):
        wait_recv(("g", q))
        start(("i", q), wg.at[q, h], wg.at[q, h], is_.at[q], ir.at[q], dev(flip=True))

    def gemm2(q):
        r, j = order[q]
        slot = {0: 0, 1: 2, 2: 1, 3: 3}[r]
        for jj in range(nj):
            arrived(slot, jj)
        wait_recv(("i", q))
        w = jnp.concatenate([wg[q, 0], wg[q, 1]], axis=1)
        p = jnp.dot(w, tall[slot], preferred_element_type=jnp.float32)
        js = slice(j * CH, (j + 1) * CH)
        if r == 0:
            out_ref[js] = p
        elif r < 3:
            out_ref[js] = out_ref[js] + p
        else:
            out_ref[js] = (out_ref[js] + p) * mask[js].astype(jnp.float32)

    def gemm2_part(own_half):
        r, j = order[last]
        js = slice(j * CH, (j + 1) * CH)
        side = h if own_half else 1 - h
        if not own_half:
            wait_recv(("i", last))
        p = jnp.dot(wg[last, side], tall[r, pl.ds(pl.multiple_of(side * vh, vh), vh)],
                    preferred_element_type=jnp.float32)
        total = out_ref[js] + p
        out_ref[js] = total if own_half else total * mask[js].astype(jnp.float32)

    def drain(q):
        for key in list(copies):
            if key[0] == "t" or key[1] <= q:
                wait_send(key)

    def prepare():
        loads[1].wait()
        mv[...] = mv[...] * mask[...]

    events = []

    def at(t, f, *args):
        events.append((t, len(events), f, args))

    unit = 3.9
    for u in range(nu):
        at(0.0, own, u)
        at(24.0 + 0.5 * unit * u, fwd, u)
    at(0.1, prepare)
    for q, (r, j) in enumerate(order):
        t = {0: 0.2 + 0.8 * j, 1: 2 * unit * (j + 1) + 2, 2: 2 * unit * (j + 1) + 2.8,
             3: nu * unit + unit * (j + 1) + 4}[r]
        if q == last:
            at(t, gemm1_unit, 0)
            at(t, gemm1_unit, 1)
        else:
            at(t, gemm1, q)
        t += LAT[0]
        at(t, scatter, q)
        if q == last:
            at(t, drain, last - 3)
        t += LAT[1]
        at(t, finish, q)
        if r > 0:
            t += LAT[2]
            if q == last:
                at(t, drain, last - 2)
            at(t, gather1, q)
        t += LAT[3]
        at(t, gather2, q)
        if q == last:
            at(t, gemm2_part, True)
        t += LAT[4]
        if r in (1, 2):
            t = max(t, unit * nu + 3)
        if q == last:
            at(t, drain, last - 1)
            at(t, gemm2_part, False)
        else:
            at(t, gemm2, q)
    for _, _, f, args in sorted(events, key=lambda e: e[:2]):
        f(*args)
    for key in copies:
        wait_send(key)


def per_device(t_amp, v_int, block_map, ny, nx):
    rows, cols = t_amp.shape
    nq = 4 * rows // CH
    vh = rows // 2
    k = CH // ny // nx
    bf, f32 = jnp.bfloat16, jnp.float32
    dma = pltpu.SemaphoreType.DMA
    vmem = pl.BlockSpec(memory_space=pltpu.VMEM)
    return pl.pallas_call(
        functools.partial(kernel, ny, nx),
        out_shape=jax.ShapeDtypeStruct((rows, cols), f32),
        in_specs=[pl.BlockSpec(memory_space=pltpu.HBM)] * 3,
        out_specs=vmem,
        scratch_shapes=[
            pltpu.VMEM((4, rows, cols), bf),
            pltpu.VMEM((rows, cols), bf),
            pltpu.VMEM((rows, cols), bf),
            pltpu.VMEM((NP, 2, CH, vh), f32),
            pltpu.VMEM((nq, CH, vh), f32),
            pltpu.VMEM((nq, CH, vh), bf),
            pltpu.VMEM((nq, ny * nx - 1, k, vh), bf),
            pltpu.VMEM((nq, k, vh), bf),
            pltpu.VMEM((nq, 2, CH, vh), bf),
            pltpu.VMEM(block_map.shape, jnp.int32),
            dma((2 + rows // UN,)), dma((4, rows // UN)), dma((4, rows // UN)),
        ] + [dma((nq + CH // UN - 1,))] * 2 + [dma((nq,))] * 8,
        compiler_params=pltpu.CompilerParams(
            collective_id=0, has_side_effects=True, vmem_limit_bytes=40 * 2**20),
        cost_estimate=pl.CostEstimate(flops=4 * rows * 4 * rows * cols, bytes_accessed=10 * rows * cols, transcendentals=0),
    )(*(pltpu.with_memory_space_constraint(a, pltpu.HBM) for a in (t_amp, v_int, block_map)))


def solution(mesh):
    spec = P("row", ("col", "cuts"))
    body = functools.partial(per_device, ny=mesh.shape["col"] // 2, nx=mesh.shape["cuts"])
    return jax.shard_map(body, mesh=mesh, in_specs=(spec,) * 3, out_specs=spec, check_vma=False)
```
